32 devices in a mesh: tile: 4 (over y, core), rep: 8 (over z, x).
Axes of the slice: x: 2, y: 2, z: 4, core: 2. Of those that a mesh axis runs over, the one named last changes fastest.
Arguments:
- inputs: bfloat16 [8, 8, 32, 32, 256], P('rep', 'tile'), may hold values from -6 to 6
- grad_out: bfloat16 [8, 8, 32, 32, 256], P('rep', 'tile'), may hold values from -6 to 6
- seam_links: int32 [8, 4, 3], P('tile'), may hold values from 0 to 7, as said below
- corner_links: int32 [8, 4, 2], P('tile'), may hold values from 0 to 7, as said below
- dw_weight: float32 [256, 9], replicated, may hold values from -1 to 1
- norm_gain: float32 [256], replicated, may hold values from 0.1 to 1.9
- w_in: bfloat16 [256, 1024], replicated, may hold values from -0.375 to 0.375
- bias_in: float32 [1024], replicated, may hold values from -1 to 1
- w_out: bfloat16 [1024, 256], replicated, may hold values from -0.1875 to 0.1875
- layer_scale: float32 [256], replicated, may hold values from 0.25 to 2
Outputs:
- block_out: bfloat16 [8, 8, 32, 32, 256], P('rep', 'tile')
- x_grad: float32 [8, 8, 32, 32, 256], P('rep', 'tile')
- grad_dw: float32 [256, 9], replicated
- grad_gain: float32 [256], replicated
- grad_w_in: float32 [256, 1024], replicated
- grad_bias: float32 [1024], replicated
- grad_w_out: float32 [1024, 256], replicated
- grad_scale: float32 [256], replicated
The draws below stay inside these ranges and needn't reach their ends.
Inputs may be any that keep to these rules, and one draw needn't show every extreme that they name: `seam_links`: entry [t, s] = (t2, s2, f): side s of tile t meets side s2 of tile t2, reversed if f = 1. Sides are paired: entry [t2, s2] = (t, s, f), and no entry names its own side. `corner_links`: entry [t, k] = (t2, k2): corner k of tile t meets corner k2 of tile t2. Corners are paired: entry [t2, k2] = (t, k), and no entry names its own corner.
All inputs are finite; a program needn't handle non-finite values.
Results may differ from the reference program's by a relative error of at most 0.0063.
Values may be sent and summed in bfloat16 or wider, within the bound.
A program may use at most 64 MiB of HBM per device.

```python
import math
import jax
import jax.numpy as jnp
from jax import lax

CHANNELS = 256
HIDDEN_UNITS = 1024
TILE_SIDE = 32
TILE_COUNT = 8
SAMPLES = 8


def paired_slots(key, slot_count):
    shuffled = jax.random.permutation(key, slot_count).astype(jnp.int32)
    leading = shuffled[0::2]
    trailing = shuffled[1::2]
    partner = jnp.zeros((slot_count,), jnp.int32).at[leading].set(trailing).at[trailing].set(leading)
    return (partner, leading, trailing)


def draw_seam_links(key, part):
    partner, leading, trailing = paired_slots(jax.random.fold_in(key, 101), TILE_COUNT * 4)
    pair_flips = jax.random.randint(jax.random.fold_in(key, 202), (TILE_COUNT * 2,), 0, 2, jnp.int32)
    flip_bits = jnp.zeros((TILE_COUNT * 4,), jnp.int32).at[leading].set(pair_flips).at[trailing].set(pair_flips)
    linked = jnp.stack([partner // 4, partner % 4, flip_bits], axis=-1)
    return linked.reshape(TILE_COUNT, 4, 3)


def draw_corner_links(key, part):
    partner, leading, trailing = paired_slots(jax.random.fold_in(key, 303), TILE_COUNT * 4)
    linked = jnp.stack([partner // 4, partner % 4], axis=-1)
    return linked.reshape(TILE_COUNT, 4, 2)


def draw_dw_weight(key, part):
    scale_key, value_key = jax.random.split(key)
    spread = jnp.exp(jax.random.uniform(scale_key, (CHANNELS, 1), jnp.float32, jnp.log(0.1), 0.0))
    values = jnp.clip(jax.random.normal(value_key, (CHANNELS, 9), jnp.float32), -2.0, 2.0) * 0.5
    return (spread * values).astype(jnp.float32)


def with_spikes(array, rng, source, target, shards_of, factor):
    def block_of(dim):
        return (jnp.arange(array.shape[dim]) // (array.shape[dim] // shards_of)).reshape((-1,) + (1,) * (array.ndim - 1 - dim))

    one_side = jax.random.permutation(rng, shards_of)[block_of(target)]
    other_side = (block_of(target) + shards_of // 2) % shards_of
    return jnp.where((block_of(source) == one_side) | (block_of(source) == other_side), factor * array, array)


def levels(key, shape, pieces, low, largest):
    level, own = 1.0, jax.random.fold_in(key, 6)
    for dim, shards_of in pieces:
        heights = jnp.exp(jax.random.uniform(jax.random.fold_in(own, dim), (shards_of,), jnp.float32, low / len(pieces), largest / len(pieces)))
        level = level * jnp.repeat(heights, shape[dim] // shards_of).reshape([-1 if axis == dim else 1 for axis in range(len(shape))])
    return level


def noise(key, shape, width, most, cuts=(), dtype=jnp.bfloat16):
    entries = width * jax.random.normal(key, shape, jnp.float32)
    if cuts:
        entries = entries * levels(key, shape, cuts, -0.22, 0.18)
    return jnp.clip(entries, -most, most).astype(dtype)


def heavy_noise(own_key, shape, scale, reach, cuts, heavy, kind=jnp.bfloat16):
    result = scale * jax.random.normal(own_key, shape, jnp.float32)
    if cuts:
        result = result * levels(own_key, shape, cuts, -0.22, 0.18)
    return jnp.clip(with_spikes(result, jax.random.fold_in(own_key, 3), *heavy), -reach, reach).astype(kind)


def setup_inputs(seed: int = 0) -> dict:
    keys = jax.random.split(jax.random.key(seed), 11)
    return {
        "inputs": heavy_noise(keys[0], (SAMPLES, TILE_COUNT, TILE_SIDE, TILE_SIDE, CHANNELS), 1.0, 6.0, ((0, 8), (1, 4)), (0, 4, 8, 2.0)),
        "grad_out": heavy_noise(keys[1], (SAMPLES, TILE_COUNT, TILE_SIDE, TILE_SIDE, CHANNELS), 1.0, 6.0, ((0, 8), (1, 4)), (1, 4, 4, 2.0)),
        "seam_links": draw_seam_links(jax.random.fold_in(keys[10], 71), 0),
        "corner_links": draw_corner_links(jax.random.fold_in(keys[10], 71), 0),
        "dw_weight": draw_dw_weight(jax.random.fold_in(keys[10], 71), 0),
        "norm_gain": jnp.clip(1.0 + 0.18 * jax.random.normal(keys[5], (CHANNELS,), jnp.float32), 0.1, 1.9),
        "w_in": noise(keys[6], (CHANNELS, HIDDEN_UNITS), CHANNELS ** -0.5, 0.375),
        "bias_in": jnp.clip(jax.random.uniform(keys[7], (HIDDEN_UNITS,), jnp.float32, -1.0, 1.0), -1.0, 1.0),
        "w_out": noise(keys[8], (HIDDEN_UNITS, CHANNELS), HIDDEN_UNITS ** -0.5, 0.1875),
        "layer_scale": jnp.clip(jnp.exp(jax.random.uniform(keys[9], (CHANNELS,), jnp.float32, math.log(0.25), math.log(2.0))), 0.25, 2.0),
    }


INV_ROOT_TWO = 0.7071067811865476
INV_ROOT_TAU = 0.3989422804014327

def edge_strips(blocks):
    top_row = blocks[..., 0, :, :]
    right_col = blocks[..., :, -1, :]
    bottom_row = blocks[..., -1, ::-1, :]
    left_col = blocks[..., ::-1, 0, :]
    return jnp.stack([top_row, right_col, bottom_row, left_col], axis=-3)

def corner_cells(blocks):
    return jnp.stack([blocks[..., 0, 0, :], blocks[..., 0, -1, :], blocks[..., -1, -1, :], blocks[..., -1, 0, :]], axis=-2)

def fetch_linked(all_strips, all_points, seam_links, corner_links):
    picked = all_strips[:, seam_links[..., 0], seam_links[..., 1]]
    reverse = (seam_links[..., 2] == 1)[None, :, :, None, None]
    strips = jnp.where(reverse, picked[..., ::-1, :], picked)
    points = all_points[:, corner_links[..., 0], corner_links[..., 1]]
    return (strips, points)

def assemble(blocks, strips, points):
    top_row = jnp.concatenate([points[..., 0:1, :], strips[..., 0, :, :], points[..., 1:2, :]], axis=-2)
    bottom_row = jnp.concatenate([points[..., 3:4, :], strips[..., 2, ::-1, :], points[..., 2:3, :]], axis=-2)
    left_col = strips[..., 3, ::-1, :][..., :, None, :]
    right_col = strips[..., 1, :, :][..., :, None, :]
    middle = jnp.concatenate([left_col, blocks, right_col], axis=-2)
    return jnp.concatenate([top_row[..., None, :, :], middle, bottom_row[..., None, :, :]], axis=-3)

def padded_parts(grad_padded):
    interior = grad_padded[..., 1:-1, 1:-1, :]
    top_row = grad_padded[..., 0, 1:-1, :]
    right_col = grad_padded[..., 1:-1, -1, :]
    bottom_row = grad_padded[..., -1, 1:-1, :][..., ::-1, :]
    left_col = grad_padded[..., 1:-1, 0, :][..., ::-1, :]
    strips = jnp.stack([top_row, right_col, bottom_row, left_col], axis=-3)
    points = jnp.stack([grad_padded[..., 0, 0, :], grad_padded[..., 0, -1, :], grad_padded[..., -1, -1, :], grad_padded[..., -1, 0, :]], axis=-2)
    return (interior, strips, points)

def add_to_rims(target, strips, points):
    extent = target.shape[-2]
    row_ids = lax.broadcasted_iota(jnp.int32, (extent, 1, 1), 0)
    col_ids = lax.broadcasted_iota(jnp.int32, (1, extent, 1), 1)
    top_mask = row_ids == 0
    bottom_mask = row_ids == extent - 1
    left_mask = col_ids == 0
    right_mask = col_ids == extent - 1
    target = target + jnp.where(top_mask, strips[..., 0, :, :][..., None, :, :], 0.0)
    target = target + jnp.where(right_mask, strips[..., 1, :, :][..., :, None, :], 0.0)
    target = target + jnp.where(bottom_mask, strips[..., 2, ::-1, :][..., None, :, :], 0.0)
    target = target + jnp.where(left_mask, strips[..., 3, ::-1, :][..., :, None, :], 0.0)
    target = target + jnp.where(top_mask & left_mask, points[..., 0, :][..., None, None, :], 0.0)
    target = target + jnp.where(top_mask & right_mask, points[..., 1, :][..., None, None, :], 0.0)
    target = target + jnp.where(bottom_mask & right_mask, points[..., 2, :][..., None, None, :], 0.0)
    target = target + jnp.where(bottom_mask & left_mask, points[..., 3, :][..., None, None, :], 0.0)
    return target

def forward_backward(padded, blocks, grad_out, dw_weight, norm_gain, w_in, bias_in, w_out, layer_scale):
    extent = blocks.shape[-2]
    channels = blocks.shape[-1]
    mixed_cells = jnp.zeros(blocks.shape, jnp.float32)
    for row_off in range(3):
        for col_off in range(3):
            tap_index = 3 * row_off + col_off
            window = padded[..., row_off:row_off + extent, col_off:col_off + extent, :].astype(jnp.float32)
            mixed_cells = mixed_cells + window * dw_weight[:, tap_index]
    average = lax.optimization_barrier(jnp.mean(mixed_cells, axis=-1, keepdims=True))
    centred = mixed_cells - average
    inv_std = lax.rsqrt(lax.optimization_barrier(jnp.mean(centred * centred, axis=-1, keepdims=True)) + 1e-06)
    standard = centred * inv_std
    normed = (standard * norm_gain).astype(jnp.bfloat16).reshape(-1, channels)
    hidden_pre = jnp.dot(normed, w_in, preferred_element_type=jnp.float32) + bias_in
    activated = jax.nn.gelu(hidden_pre, approximate=False).astype(jnp.bfloat16)
    branch = jnp.dot(activated, w_out, preferred_element_type=jnp.float32)
    cotangent = grad_out.reshape(-1, channels).astype(jnp.float32)
    block_out = (blocks.reshape(-1, channels).astype(jnp.float32) + layer_scale * branch).astype(jnp.bfloat16).reshape(blocks.shape)
    grad_scale = lax.optimization_barrier(jnp.sum(cotangent * branch, axis=0))
    grad_mix = (cotangent * layer_scale).astype(jnp.bfloat16)
    grad_w_out = lax.dot_general(activated, grad_mix, (((0,), (0,)), ((), ())), preferred_element_type=jnp.float32)
    grad_act = lax.dot_general(grad_mix, w_out, (((1,), (1,)), ((), ())), preferred_element_type=jnp.float32)
    gelu_slope = 0.5 * (1.0 + lax.erf(hidden_pre * INV_ROOT_TWO)) + hidden_pre * jnp.exp(-0.5 * hidden_pre * hidden_pre) * INV_ROOT_TAU
    grad_hidden = (grad_act * gelu_slope).astype(jnp.bfloat16)
    grad_bias = lax.optimization_barrier(jnp.sum(grad_hidden.astype(jnp.float32), axis=0))
    grad_w_in = lax.dot_general(normed, grad_hidden, (((0,), (0,)), ((), ())), preferred_element_type=jnp.float32)
    grad_normed = lax.dot_general(grad_hidden, w_in, (((1,), (1,)), ((), ())), preferred_element_type=jnp.float32).reshape(blocks.shape)
    grad_gain = lax.optimization_barrier(jnp.sum((grad_normed * standard).reshape(-1, channels), axis=0))
    grad_unit = grad_normed * norm_gain
    grad_mixed = (grad_unit - lax.optimization_barrier(jnp.mean(grad_unit, axis=-1, keepdims=True)) - standard * lax.optimization_barrier(jnp.mean(grad_unit * standard, axis=-1, keepdims=True))) * inv_std
    pad_widths = [(0, 0)] * (grad_mixed.ndim - 3) + [(2, 2), (2, 2), (0, 0)]
    wide_grad = jnp.pad(grad_mixed, pad_widths)
    grad_padded = jnp.zeros(padded.shape, jnp.float32)
    dw_columns = []
    for row_off in range(3):
        for col_off in range(3):
            tap_index = 3 * row_off + col_off
            window = padded[..., row_off:row_off + extent, col_off:col_off + extent, :].astype(jnp.float32)
            shifted = wide_grad[..., 2 - row_off:4 - row_off + extent, 2 - col_off:4 - col_off + extent, :]
            grad_padded = grad_padded + shifted * dw_weight[:, tap_index]
            dw_columns.append(lax.optimization_barrier(jnp.sum((grad_mixed * window).reshape(-1, channels), axis=0)))
    grad_dw = jnp.stack(dw_columns, axis=1)
    return (block_out, grad_padded, (grad_dw, grad_gain, grad_w_in, grad_bias, grad_w_out, grad_scale))

def reference(inputs, grad_out, seam_links, corner_links, dw_weight, norm_gain, w_in, bias_in, w_out, layer_scale):
    strips, points = fetch_linked(edge_strips(inputs), corner_cells(inputs), seam_links, corner_links)
    padded = assemble(inputs, strips, points)

    def per_sample(sample_items):
        padded_one, blocks, cotangent = sample_items
        return forward_backward(padded_one, blocks, cotangent, dw_weight, norm_gain, w_in, bias_in, w_out, layer_scale)
    block_out, grad_padded, partials = lax.map(per_sample, (padded, inputs, grad_out))
    interior, back_strips, back_points = padded_parts(grad_padded)
    home_strips, home_points = fetch_linked(back_strips, back_points, seam_links, corner_links)
    x_grad = add_to_rims(grad_out.astype(jnp.float32) + interior, home_strips, home_points)
    factor = 1.0 / math.sqrt(SAMPLES * TILE_COUNT * TILE_SIDE * TILE_SIDE)
    totals = [lax.optimization_barrier(jnp.sum(partial_sum, axis=0)) * factor for partial_sum in partials]
    return (block_out, x_grad, totals[0], totals[1], totals[2], totals[3], totals[4], totals[5])
```

```python
import functools
import math

import jax
import jax.numpy as jnp
from jax import lax
from jax.experimental import pallas as pl
from jax.experimental.pallas import tpu as pltpu
from jax.sharding import PartitionSpec as P

INV_ROOT_TWO = 0.7071067811865476
INV_ROOT_TAU = 0.3989422804014327
MESH = pl.DeviceIdType.MESH
F32 = jnp.float32
BF16 = jnp.bfloat16
VMEM = pl.BlockSpec(memory_space=pltpu.VMEM)
SMEM = pl.BlockSpec(memory_space=pltpu.SMEM)
NN = (((1,), (0,)), ((), ()))
NT = (((1,), (1,)), ((), ()))
TN = (((0,), (0,)), ((), ()))
SIDES = 4
CORNER_ROWS = 16


def dot(a, b, dims=NN):
    return lax.dot_general(a, b, dims, preferred_element_type=F32)


def iota(shape, dim):
    return lax.broadcasted_iota(jnp.int32, shape, dim)


def one_hot(mask):
    return jnp.where(mask, 1.0, 0.0).astype(BF16)


def tile_gather(tiles, buf, send_sem, recv_sem):
    size = lax.axis_size("tile")
    me = lax.axis_index("tile")
    mine = pl.ds(me * tiles, tiles)
    copies = []
    for k in range(1, size):
        copy = pltpu.make_async_remote_copy(
            src_ref=buf.at[mine],
            dst_ref=buf.at[mine],
            send_sem=send_sem.at[k - 1],
            recv_sem=recv_sem.at[k - 1],
            device_id={"tile": lax.rem(me + k, size)},
            device_id_type=MESH,
        )
        copy.start()
        copies.append(copy)
    return copies


def halo_kernel(side, tiles, x_ref, out_ref, land, send_sem, recv_sem):
    size = lax.axis_size("tile")
    me = lax.axis_index("tile")
    barrier = pltpu.get_barrier_semaphore()
    for k in range(1, size):
        pl.semaphore_signal(
            barrier, inc=1, device_id={"tile": lax.rem(me + k, size)}, device_id_type=MESH
        )
    rows = SIDES * side
    cells = side * side
    r = iota((rows, cells), 0)
    c = iota((rows, cells), 1)
    s = r // side
    p = r % side
    target = jnp.where(
        s == 0,
        p,
        jnp.where(
            s == 1,
            p * side + side - 1,
            jnp.where(s == 2, (side - 1) * side + p, p * side),
        ),
    )
    sel = one_hot(c == target)
    for t in range(tiles):
        land[me * tiles + t] = dot(sel, x_ref[t]).astype(BF16)
    pl.semaphore_wait(barrier, size - 1)
    copies = tile_gather(tiles, land, send_sem, recv_sem)
    for copy in copies:
        copy.wait()
    out_ref[...] = land[...]


def gather_halos(x):
    tiles, cells, channels = x.shape
    side = math.isqrt(cells)
    size = lax.axis_size("tile")
    shape = (size * tiles, SIDES * side, channels)
    return pl.pallas_call(
        functools.partial(halo_kernel, side, tiles),
        out_shape=jax.ShapeDtypeStruct(shape, BF16),
        in_specs=[VMEM],
        out_specs=VMEM,
        scratch_shapes=[
            pltpu.VMEM(shape, BF16),
            pltpu.SemaphoreType.DMA((size - 1,)),
            pltpu.SemaphoreType.DMA((size - 1,)),
        ],
        compiler_params=pltpu.CompilerParams(
            collective_id=0, has_side_effects=True, vmem_limit_bytes=32 * 2**20
        ),
        name="halo_gather",
    )(x)


def compute_kernel(
    side,
    tiles,
    seam_ref,
    corner_ref,
    strips_ref,
    x_ref,
    g_ref,
    dw_ref,
    gain_ref,
    w_in_ref,
    bias_ref,
    w_out_ref,
    scale_ref,
    out_ref,
    xg_ref,
    back_ref,
    acc_ref,
    small_ref,
    xs,
    gm_buf,
    strip_buf,
    dw_acc,
    vec_acc,
    bias_acc,
):
    channels = x_ref.shape[-1]
    hidden = w_in_ref.shape[1]
    ext = side + 2
    last = side - 1
    gain = gain_ref[...]
    scale = scale_ref[...]
    chunk_rows = 8
    n = chunk_rows * side
    hb = 256
    lanes = 128

    dw_acc[...] = jnp.zeros_like(dw_acc)
    vec_acc[...] = jnp.zeros_like(vec_acc)
    bias_acc[...] = jnp.zeros_like(bias_acc)
    acc_ref[...] = jnp.zeros_like(acc_ref)
    small_ref[...] = jnp.zeros_like(small_ref)
    strip_buf[...] = jnp.zeros_like(strip_buf)

    for t in range(tiles):
        picks = []
        flips = []
        for s in range(SIDES):
            t2, s2, f = seam_ref[t, s, 0], seam_ref[t, s, 1], seam_ref[t, s, 2]
            flip = lax.rem(f + (1 if s >= 2 else 0) + jnp.where(s2 >= 2, 1, 0), 2)
            picks.append(strips_ref[t2, pl.ds(pl.multiple_of(s2 * side, side), side), :])
            flips.append(flip)
        corner_rows = []
        for k in range(4):
            t2, k2 = corner_ref[t, k, 0], corner_ref[t, k, 1]
            picks.append(strips_ref[t2, pl.ds(pl.multiple_of(k2 * side, side), side), :])
            corner_rows.append(jnp.where(k2 >= 2, last, 0))
        table = jnp.concatenate(picks, axis=0)

        def place(p, s):
            return s * side + p + flips[s] * (last - 2 * p)

        def corner_place(k):
            return SIDES * side + k * side + corner_rows[k]

        p = iota((side, 2 * SIDES * side), 0)
        r = iota((side, 2 * SIDES * side), 1)
        xs[1, t, 0:side, :] = dot(one_hot(r == place(p, 0)), table)
        xs[1, t, (ext - 1) * side :, :] = dot(one_hot(r == place(p, 2)), table)
        xs[1, t, side : (ext - 1) * side, :] = x_ref[t].astype(F32)
        half = ext // 2 * side

        def shift_rows(h, _, t=t):
            start = pl.multiple_of(h * half, side)
            rows = xs[1, t, pl.ds(start, half), :]
            cell = start + iota((half, 1), 0)
            i = cell // side - 1
            j = cell % side
            rr = iota((half, 2 * SIDES * side), 1)

            def column(sd, k_top, k_bottom):
                return jnp.where(
                    i < 0,
                    corner_place(k_top),
                    jnp.where(i > last, corner_place(k_bottom), place(i, sd)),
                )

            left = jnp.where(j == 0, column(3, 0, 3), -1)
            right = jnp.where(j == last, column(1, 1, 2), -1)
            ins_left = dot(one_hot(rr == left), table)
            ins_right = dot(one_hot(rr == right), table)
            xs[0, t, pl.ds(start, half), :] = jnp.where(j == 0, ins_left, pltpu.roll(rows, 1, 0))
            xs[2, t, pl.ds(start, half), :] = jnp.where(
                j == last, ins_right, pltpu.roll(rows, half - 1, 0)
            )
            return 0

        lax.fori_loop(0, 2, shift_rows, 0)
        gm_buf[t, 0:side, :] = jnp.zeros((side, channels), F32)
        gm_buf[t, (ext - 1) * side :, :] = jnp.zeros((side, channels), F32)

    chunks = side // chunk_rows

    def fold(v):
        return jnp.sum(v.reshape(v.shape[0] // 8, 8, v.shape[1]), axis=0)

    def step(idx, _):
        t = idx // chunks
        base = pl.multiple_of(lax.rem(idx, chunks) * n, n)
        mixed = jnp.zeros((n, channels), F32)
        for a in range(3):
            for b in range(3):
                w = dw_ref[3 * a + b : 3 * a + b + 1, :]
                mixed = mixed + xs[b, t, pl.ds(base + a * side, n), :] * w
        mean = jnp.mean(mixed, axis=-1, keepdims=True)
        centred = mixed - mean
        inv_std = lax.rsqrt(jnp.mean(centred * centred, axis=-1, keepdims=True) + 1e-06)
        unit = centred * inv_std
        normed = (unit * gain).astype(BF16)
        g = g_ref[t, pl.ds(base, n), :].astype(F32)
        mix = (g * scale).astype(BF16)
        branch = jnp.zeros((n, channels), F32)
        gn = jnp.zeros((n, channels), F32)
        for h in range(hidden // hb):
            cols = slice(h * hb, (h + 1) * hb)
            pre = dot(normed, w_in_ref[:, cols]) + bias_ref[:, cols]
            phi_cum = 0.5 * (1.0 + lax.erf(pre * INV_ROOT_TWO))
            act = (pre * phi_cum).astype(BF16)
            slope = phi_cum + pre * jnp.exp(-0.5 * pre * pre) * INV_ROOT_TAU
            gact = dot(mix, w_out_ref[cols, :], NT)
            ghf = (gact * slope).astype(BF16)
            branch = branch + dot(act, w_out_ref[cols, :])
            gn = gn + dot(ghf, w_in_ref[:, cols], NT)
            bias_acc[:, cols] += fold(ghf.astype(F32))
            gwi = dot(normed, ghf, TN)
            gwo = dot(mix, act, TN)
            for q in range(hb // lanes):
                blk = h * (hb // lanes) + q
                acc_ref[blk] += gwi[:, q * lanes : (q + 1) * lanes]
                acc_ref[hidden // lanes + blk] += gwo[:, q * lanes : (q + 1) * lanes]
        x = x_ref[t, pl.ds(base, n), :].astype(F32)
        out_ref[t, pl.ds(base, n), :] = (x + scale * branch).astype(BF16)
        vec_acc[0] += fold(gn * unit)
        vec_acc[1] += fold(g * branch)
        u = gn * gain
        gm = (
            u
            - jnp.mean(u, axis=-1, keepdims=True)
            - unit * jnp.mean(u * unit, axis=-1, keepdims=True)
        ) * inv_std
        gm_buf[t, pl.ds(base + side, n), :] = gm
        for a in range(3):
            for b in range(3):
                dw_acc[3 * a + b] += fold(gm * xs[b, t, pl.ds(base + a * side, n), :])
        return 0

    lax.fori_loop(0, tiles * chunks, step, 0)

    def taps(t, start, size, b):
        total = jnp.zeros((size, channels), F32)
        for a in range(3):
            w = dw_ref[3 * a + b : 3 * a + b + 1, :]
            total = total + gm_buf[t, pl.ds(start + (2 - a) * side, size), :] * w
        return total

    def back_step(idx, _):
        t = idx // chunks
        c = lax.rem(idx, chunks)
        base = pl.multiple_of(c * n, n)
        j = iota((n, 1), 0) % side
        left = taps(t, base, n, 0)
        right = taps(t, base, n, 2)
        grad = g_ref[t, pl.ds(base, n), :].astype(F32) + taps(t, base, n, 1)
        grad = grad + jnp.where(j == last, 0.0, pltpu.roll(left, n - 1, 0))
        grad = grad + jnp.where(j == 0, 0.0, pltpu.roll(right, 1, 0))
        xg_ref[t, pl.ds(base, n), :] = grad
        ri = iota((chunk_rows, n), 0)
        ci = iota((chunk_rows, n), 1)
        row0 = pl.multiple_of(c * chunk_rows, chunk_rows)
        strip_buf[t, pl.ds(3 * side + row0, chunk_rows), :] = dot(
            one_hot(ci == ri * side), left.astype(BF16)
        )
        strip_buf[t, pl.ds(side + row0, chunk_rows), :] = dot(
            one_hot(ci == ri * side + last), right.astype(BF16)
        )
        return 0

    lax.fori_loop(0, tiles * chunks, back_step, 0)
    j = iota((side, 1), 0)
    for t in range(tiles):
        for s, a, row in ((0, 0, 1), (2, 2, side)):
            edge = gm_buf[t, row * side : (row + 1) * side, :]
            left = edge * dw_ref[3 * a : 3 * a + 1, :]
            mid = edge * dw_ref[3 * a + 1 : 3 * a + 2, :]
            right = edge * dw_ref[3 * a + 2 : 3 * a + 3, :]
            mid = mid + jnp.where(j == last, 0.0, pltpu.roll(left, side - 1, 0))
            mid = mid + jnp.where(j == 0, 0.0, pltpu.roll(right, 1, 0))
            strip_buf[t, s * side : (s + 1) * side, :] = mid
            k_left, k_right = (0, 1) if s == 0 else (3, 2)
            at = SIDES * side
            strip_buf[t, at + k_left : at + k_left + 1, :] = left[0:1, :]
            strip_buf[t, at + k_right : at + k_right + 1, :] = right[last : last + 1, :]
    back_ref[...] = strip_buf[...].astype(BF16)
    for k in range(9):
        small_ref[k : k + 1, :] = jnp.sum(dw_acc[k], axis=0, keepdims=True)
    for k in range(2):
        small_ref[9 + k : 10 + k, :] = jnp.sum(vec_acc[k], axis=0, keepdims=True)
    for k in range(hidden // channels):
        small_ref[11 + k : 12 + k, :] = jnp.sum(
            bias_acc[:, k * channels : (k + 1) * channels], axis=0, keepdims=True
        )


def compute(seam, corner, strips, x, g, dw, gain, w_in, bias, w_out, scale):
    tiles, cells, channels = x.shape
    side = math.isqrt(cells)
    hidden = w_in.shape[1]
    ext = side + 2
    return pl.pallas_call(
        functools.partial(compute_kernel, side, tiles),
        out_shape=(
            jax.ShapeDtypeStruct(x.shape, BF16),
            jax.ShapeDtypeStruct(x.shape, F32),
            jax.ShapeDtypeStruct((tiles, SIDES * side + CORNER_ROWS, channels), BF16),
            jax.ShapeDtypeStruct((2 * hidden // 128, channels, 128), F32),
            jax.ShapeDtypeStruct((16, channels), F32),
        ),
        in_specs=[SMEM, SMEM] + [VMEM] * 9,
        out_specs=(VMEM,) * 5,
        scratch_shapes=[
            pltpu.VMEM((3, tiles, ext * side, channels), F32),
            pltpu.VMEM((tiles, ext * side, channels), F32),
            pltpu.VMEM((tiles, SIDES * side + CORNER_ROWS, channels), F32),
            pltpu.VMEM((9, 8, channels), F32),
            pltpu.VMEM((2, 8, channels), F32),
            pltpu.VMEM((8, hidden), F32),
        ],
        compiler_params=pltpu.CompilerParams(vmem_limit_bytes=50 * 2**20),
        name="block_grads",
    )(seam, corner, strips, x, g, dw, gain, w_in, bias, w_out, scale)


def digits_of(tile_size, rep_size):
    low = 2 ** (int(math.log2(rep_size)) // 2)
    core = ("tile", 1, 2)
    rest = ("tile", 2, tile_size // 2)
    near = ("rep", 1, low)
    far = ("rep", low, rep_size // low)
    return core, rest, near, far


def finish_kernel(
    side,
    tiles,
    factor,
    orders,
    seam_ref,
    corner_ref,
    xg_in,
    back_ref,
    acc_ref,
    small_ref,
    xg_ref,
    gwi_ref,
    gwo_ref,
    tot_ref,
    land,
    cur,
    snd,
    rcv,
    full,
    small_slots,
    halo_send,
    halo_recv,
    rs_send,
    rs_recv,
    ag_send,
    ag_recv,
    sm_send,
    sm_recv,
):
    tile_size = lax.axis_size("tile")
    rep_size = lax.axis_size("rep")
    index = {"tile": lax.axis_index("tile"), "rep": lax.axis_index("rep")}
    core, rest, near, far = digits_of(tile_size, rep_size)
    pieces = acc_ref.shape[0]
    part_size = pieces // len(orders)
    last = side - 1

    def digit(d):
        axis, stride, size = d
        return lax.rem(index[axis] // stride, size)

    def peer(d, value):
        axis, stride, size = d
        return {axis: index[axis] + (value - digit(d)) * stride}

    barrier = pltpu.get_barrier_semaphore()
    signals = 0
    for k in range(1, tile_size):
        pl.semaphore_signal(
            barrier,
            inc=1,
            device_id={"tile": lax.rem(index["tile"] + k, tile_size)},
            device_id_type=MESH,
        )
        signals += 1
    for d in (near, far):
        for k in range(1, d[2]):
            pl.semaphore_signal(
                barrier,
                inc=1,
                device_id=peer(d, lax.rem(digit(d) + k, d[2])),
                device_id_type=MESH,
            )
            signals += 1
    pl.semaphore_wait(barrier, signals)

    land[pl.ds(index["tile"] * tiles, tiles)] = back_ref[...]

    offsets = []
    for part, order in enumerate(orders):
        off = part * part_size
        size = part_size
        stages = []
        for d in order:
            size = size // d[2]
            stages.append((off, size))
            off = off + digit(d) * size
        stages.append((off, size))
        offsets.append(stages)
    sem_at = {}
    rcv_at = {}
    sems = 0
    rows = 0
    for part, order in enumerate(orders):
        for s, d in enumerate(order):
            sem_at[part, s] = sems
            rcv_at[part, s] = rows
            sems += d[2] - 1
            rows += (d[2] - 1) * offsets[part][s][1]

    def start_scatter(part, s):
        d = orders[part][s]
        off, size = offsets[part][s]
        src = acc_ref if s == 0 else cur
        copies = []
        for k in range(1, d[2]):
            to = lax.rem(digit(d) + k, d[2])
            where = pl.ds(off + to * size, size)
            snd[where] = src[where].astype(BF16)
            copy = pltpu.make_async_remote_copy(
                src_ref=snd.at[where],
                dst_ref=rcv.at[pl.ds(rcv_at[part, s] + (k - 1) * size, size)],
                send_sem=rs_send.at[sem_at[part, s] + k - 1],
                recv_sem=rs_recv.at[sem_at[part, s] + k - 1],
                device_id=peer(d, to),
                device_id_type=MESH,
            )
            copy.start()
            copies.append(copy)
        return copies

    def end_scatter(part, s, copies):
        d = orders[part][s]
        _, size = offsets[part][s]
        off, _ = offsets[part][s + 1]
        src = acc_ref if s == 0 else cur
        total = src[pl.ds(off, size)]
        for k, copy in enumerate(copies):
            copy.wait_recv()
            total = total + rcv[pl.ds(rcv_at[part, s] + k * size, size)].astype(F32)
        if s == len(orders[part]) - 1:
            full[pl.ds(off, size)] = (total * factor).astype(BF16)
        else:
            cur[pl.ds(off, size)] = total

    def start_gather(part, s):
        d = orders[part][s]
        off, size = offsets[part][s + 1][0], offsets[part][s][1]
        copies = []
        for k in range(1, d[2]):
            to = lax.rem(digit(d) + k, d[2])
            copy = pltpu.make_async_remote_copy(
                src_ref=full.at[pl.ds(off, size)],
                dst_ref=full.at[pl.ds(off, size)],
                send_sem=ag_send.at[sem_at[part, s] + k - 1],
                recv_sem=ag_recv.at[sem_at[part, s] + k - 1],
                device_id=peer(d, to),
                device_id_type=MESH,
            )
            copy.start()
            copies.append(copy)
        return copies

    small_order = orders[0]
    small_base = [0]
    small_sem = [0]
    for d in small_order:
        small_base.append(small_base[-1] + d[2])
        small_sem.append(small_sem[-1] + d[2] - 1)

    def start_small(s, value):
        d = small_order[s]
        mine = small_base[s] + digit(d)
        small_slots[mine] = value
        copies = []
        for k in range(1, d[2]):
            to = lax.rem(digit(d) + k, d[2])
            copy = pltpu.make_async_remote_copy(
                src_ref=small_slots.at[mine],
                dst_ref=small_slots.at[mine],
                send_sem=sm_send.at[small_sem[s] + k - 1],
                recv_sem=sm_recv.at[small_sem[s] + k - 1],
                device_id=peer(d, to),
                device_id_type=MESH,
            )
            copy.start()
            copies.append(copy)
        return copies

    def end_small(s, copies):
        for copy in copies:
            copy.wait_recv()
        total = small_slots[small_base[s]]
        for k in range(1, small_order[s][2]):
            total = total + small_slots[small_base[s] + k]
        return total

    every = []
    stage_count = len(small_order)
    part_ids = range(len(orders))
    flying = {}
    for part in part_ids:
        flying[part] = start_scatter(part, 0)
        every += flying[part]
    halo = tile_gather(tiles, land, halo_send, halo_recv)
    small = start_small(0, small_ref[...])
    every += small
    for s in range(stage_count):
        for part in part_ids:
            end_scatter(part, s, flying[part])
            if s + 1 < stage_count:
                flying[part] = start_scatter(part, s + 1)
            else:
                flying[part] = start_gather(part, s)
            every += flying[part]
        value = end_small(s, small)
        if s + 1 < stage_count:
            small = start_small(s + 1, value)
            every += small
    tot_ref[...] = value * factor

    for copy in halo:
        copy.wait()
    cells = side * side
    width = SIDES * side + CORNER_ROWS
    total_rows = land.shape[0] * width
    home = land[...].reshape(total_rows, land.shape[2])
    row = iota((width, 1), 0)
    rr = iota((width, total_rows), 1)
    cell = iota((cells, 1), 0)
    i = cell // side
    j = cell % side
    r = iota((cells, width), 1)
    rim = None
    for s, (on, p) in enumerate(((i == 0, j), (j == last, i), (i == last, j), (j == 0, i))):
        hit = r == jnp.where(on, s * side + p, -1)
        rim = hit if rim is None else rim | hit
    for k, cell_k in enumerate((0, last, cells - 1, cells - side)):
        rim = rim | (r == jnp.where(cell == cell_k, SIDES * side + k, -1))
    rim = one_hot(rim)
    for t in range(tiles):
        source = jnp.full((width, 1), -1, jnp.int32)
        for s in range(SIDES):
            t2, s2, f = seam_ref[t, s, 0], seam_ref[t, s, 1], seam_ref[t, s, 2]
            flip = f + (1 if s >= 2 else 0) + s2 // 2
            flip = flip - 2 * (flip // 2)
            p = row - s * side
            at = t2 * width + s2 * side + p + flip * (last - 2 * p)
            source = jnp.where((row >= s * side) & (row < (s + 1) * side), at, source)
        for k in range(4):
            t2, k2 = corner_ref[t, k, 0], corner_ref[t, k, 1]
            at = t2 * width + SIDES * side + k2
            source = jnp.where(row == SIDES * side + k, at, source)
        table = dot(one_hot(rr == source), home).astype(BF16)
        xg_ref[t] = xg_in[t] + dot(rim, table)

    for s in reversed(range(stage_count)):
        for part in part_ids:
            for copy in flying[part]:
                copy.wait_recv()
            if s > 0:
                flying[part] = start_gather(part, s - 1)
                every += flying[part]
    channels = gwi_ref.shape[0]
    hidden = gwi_ref.shape[1]
    per = channels // 16
    for h in range(hidden // 128):
        block = full[pl.ds(h * per, per)].astype(F32).reshape(channels, 128)
        gwi_ref[:, h * 128 : (h + 1) * 128] = block
        at = (hidden // 128 + h) * per
        block = full[pl.ds(at, per)].astype(F32).reshape(channels, 128)
        gwo_ref[h * 128 : (h + 1) * 128, :] = block.T
    for copy in every:
        copy.wait_send()


def finish(seam, corner, xg, back, acc, small, factor):
    tiles, cells, channels = xg.shape
    side = math.isqrt(cells)
    tile_size = lax.axis_size("tile")
    rep_size = lax.axis_size("rep")
    acc = acc.reshape(-1, 16, 128)
    hidden = acc.shape[0] * 16 * 128 // (2 * channels)
    core, rest, near, far = digits_of(tile_size, rep_size)
    orders = [(core, rest, near, far), (core, near, rest, far)]
    if acc.shape[0] < 2 * tile_size * rep_size:
        orders = orders[:1]
    sems = 0
    rows = 0
    for order in orders:
        size = acc.shape[0] // len(orders)
        for d in order:
            size = size // d[2]
            sems += d[2] - 1
            rows += (d[2] - 1) * size
    slots = sum(d[2] for d in orders[0])
    dma = pltpu.SemaphoreType.DMA
    return pl.pallas_call(
        functools.partial(finish_kernel, side, tiles, factor, orders),
        out_shape=(
            jax.ShapeDtypeStruct(xg.shape, F32),
            jax.ShapeDtypeStruct((channels, hidden), F32),
            jax.ShapeDtypeStruct((hidden, channels), F32),
            jax.ShapeDtypeStruct(small.shape, F32),
        ),
        in_specs=[SMEM, SMEM] + [VMEM] * 4,
        out_specs=(VMEM,) * 4,
        scratch_shapes=[
            pltpu.VMEM((tile_size * tiles,) + back.shape[1:], BF16),
            pltpu.VMEM(acc.shape, F32),
            pltpu.VMEM(acc.shape, BF16),
            pltpu.VMEM((rows, 16, 128), BF16),
            pltpu.VMEM(acc.shape, BF16),
            pltpu.VMEM((slots,) + small.shape, F32),
            dma((tile_size - 1,)),
            dma((tile_size - 1,)),
            dma((sems,)),
            dma((sems,)),
            dma((sems,)),
            dma((sems,)),
            dma((slots,)),
            dma((slots,)),
        ],
        compiler_params=pltpu.CompilerParams(
            collective_id=1, has_side_effects=True, vmem_limit_bytes=50 * 2**20
        ),
        name="grad_sum",
    )(seam, corner, xg, back, acc, small)


def body(
    inputs,
    grad_out,
    seam_links,
    corner_links,
    dw_weight,
    norm_gain,
    w_in,
    bias_in,
    w_out,
    layer_scale,
):
    samples, local, side, _, channels = inputs.shape
    tiles = samples * local
    x = inputs.reshape(tiles, side * side, channels)
    g = grad_out.reshape(tiles, side * side, channels)
    cell_total = lax.axis_size("tile") * lax.axis_size("rep") * tiles * side * side
    factor = 1.0 / math.sqrt(cell_total)
    strips = gather_halos(x)
    out, xg, back, acc, small = compute(
        seam_links,
        corner_links,
        strips,
        x,
        g,
        dw_weight.T,
        norm_gain[None],
        w_in,
        bias_in[None],
        w_out,
        layer_scale[None],
    )
    xg, gwi, gwo, total = finish(seam_links, corner_links, xg, back, acc, small, factor)
    return (
        out.reshape(inputs.shape),
        xg.reshape(inputs.shape),
        total[0:9].T,
        total[9],
        gwi,
        total[11 : 11 + w_in.shape[1] // channels].reshape(-1),
        gwo,
        total[10],
    )


def solution(mesh):
    placed = (
        P("rep", "tile", None, None, None),
        P("rep", "tile", None, None, None),
        P("tile", None, None),
        P("tile", None, None),
        P(),
        P(),
        P(),
        P(),
        P(),
        P(),
    )
    return jax.shard_map(
        body,
        mesh=mesh,
        in_specs=placed,
        out_specs=(
            P("rep", "tile", None, None, None),
            P("rep", "tile", None, None, None),
            P(),
            P(),
            P(),
            P(),
            P(),
            P(),
        ),
        check_vma=False,
    )
```

```python
import functools
import math

import jax
import jax.numpy as jnp
from jax import lax
from jax.experimental import pallas as pl
from jax.experimental.pallas import tpu as pltpu
from jax.sharding import PartitionSpec as P

INV_ROOT_TWO = 0.7071067811865476
INV_ROOT_TAU = 0.3989422804014327
MESH = pl.DeviceIdType.MESH
F32 = jnp.float32
BF16 = jnp.bfloat16
VMEM = pl.BlockSpec(memory_space=pltpu.VMEM)
SMEM = pl.BlockSpec(memory_space=pltpu.SMEM)
NN = (((1,), (0,)), ((), ()))
NT = (((1,), (1,)), ((), ()))
TN = (((0,), (0,)), ((), ()))
SIDES = 4
CORNER_ROWS = 16


def dot(a, b, dims=NN):
    return lax.dot_general(a, b, dims, preferred_element_type=F32)


def iota(shape, dim):
    return lax.broadcasted_iota(jnp.int32, shape, dim)


def one_hot(mask):
    return jnp.where(mask, 1.0, 0.0).astype(BF16)


def block_copy(tiles, buf, send_sem, recv_sem, block, to, slot):
    where = pl.ds(block * tiles, tiles)
    copy = pltpu.make_async_remote_copy(
        src_ref=buf.at[where],
        dst_ref=buf.at[where],
        send_sem=send_sem.at[slot],
        recv_sem=recv_sem.at[slot],
        device_id={"tile": to},
        device_id_type=MESH,
    )
    copy.start()
    return copy


def tile_gather(*refs):
    size = lax.axis_size("tile")
    me = lax.axis_index("tile")
    far = [
        block_copy(*refs, me, lax.rem(me + 2 * k, size), k - 1) for k in range(1, size // 2)
    ]
    near = block_copy(*refs, me, me + 1 - 2 * lax.rem(me, 2), size // 2 - 1)
    return far, near


def tile_forward(started, *refs):
    size = lax.axis_size("tile")
    me = lax.axis_index("tile")
    far, near = started
    passed = []
    for k, copy in enumerate(far, 1):
        copy.wait_recv()
        block = lax.rem(me + size - 2 * k, size)
        passed.append(
            block_copy(*refs, block, me + 1 - 2 * lax.rem(me, 2), size // 2 - 1 + k)
        )
    return far, [near] + passed


def tile_end(far, near):
    for copy in near:
        copy.wait_recv()
    for copy in far + near:
        copy.wait_send()


def halo_kernel(side, tiles, x_ref, out_ref, land, send_sem, recv_sem):
    size = lax.axis_size("tile")
    me = lax.axis_index("tile")
    barrier = pltpu.get_barrier_semaphore()
    for k in range(1, size):
        pl.semaphore_signal(
            barrier, inc=1, device_id={"tile": lax.rem(me + k, size)}, device_id_type=MESH
        )
    rows = SIDES * side
    cells = side * side
    r = iota((rows, cells), 0)
    c = iota((rows, cells), 1)
    s = r // side
    p = r % side
    target = jnp.where(
        s == 0,
        p,
        jnp.where(
            s == 1,
            p * side + side - 1,
            jnp.where(s == 2, (side - 1) * side + p, p * side),
        ),
    )
    sel = one_hot(c == target)
    for t in range(tiles):
        land[me * tiles + t] = dot(sel, x_ref[t]).astype(BF16)
    pl.semaphore_wait(barrier, size - 1)
    refs = (tiles, land, send_sem, recv_sem)
    tile_end(*tile_forward(tile_gather(*refs), *refs))
    out_ref[...] = land[...]


def gather_halos(x):
    tiles, cells, channels = x.shape
    side = math.isqrt(cells)
    size = lax.axis_size("tile")
    shape = (size * tiles, SIDES * side, channels)
    return pl.pallas_call(
        functools.partial(halo_kernel, side, tiles),
        out_shape=jax.ShapeDtypeStruct(shape, BF16),
        in_specs=[VMEM],
        out_specs=VMEM,
        scratch_shapes=[
            pltpu.VMEM(shape, BF16),
            pltpu.SemaphoreType.DMA((size - 1,)),
            pltpu.SemaphoreType.DMA((size - 1,)),
        ],
        compiler_params=pltpu.CompilerParams(
            collective_id=0, has_side_effects=True, vmem_limit_bytes=32 * 2**20
        ),
        name="halo_gather",
    )(x)


def compute_kernel(
    side,
    tiles,
    seam_ref,
    corner_ref,
    strips_ref,
    x_ref,
    g_ref,
    dw_ref,
    gain_ref,
    w_in_ref,
    bias_ref,
    w_out_ref,
    scale_ref,
    out_ref,
    xg_ref,
    back_ref,
    acc_ref,
    small_ref,
    xs,
    gm_buf,
    strip_buf,
    dw_acc,
    vec_acc,
    bias_acc,
):
    channels = x_ref.shape[-1]
    hidden = w_in_ref.shape[1]
    ext = side + 2
    last = side - 1
    gain = gain_ref[...]
    scale = scale_ref[...]
    chunk_rows = 8
    n = chunk_rows * side
    hb = 256
    lanes = 128

    dw_acc[...] = jnp.zeros_like(dw_acc)
    vec_acc[...] = jnp.zeros_like(vec_acc)
    bias_acc[...] = jnp.zeros_like(bias_acc)
    acc_ref[...] = jnp.zeros_like(acc_ref)
    small_ref[...] = jnp.zeros_like(small_ref)
    strip_buf[...] = jnp.zeros_like(strip_buf)

    for t in range(tiles):
        picks = []
        flips = []
        for s in range(SIDES):
            t2, s2, f = seam_ref[t, s, 0], seam_ref[t, s, 1], seam_ref[t, s, 2]
            flip = lax.rem(f + (1 if s >= 2 else 0) + jnp.where(s2 >= 2, 1, 0), 2)
            picks.append(strips_ref[t2, pl.ds(pl.multiple_of(s2 * side, side), side), :])
            flips.append(flip)
        corner_rows = []
        for k in range(4):
            t2, k2 = corner_ref[t, k, 0], corner_ref[t, k, 1]
            picks.append(strips_ref[t2, pl.ds(pl.multiple_of(k2 * side, side), side), :])
            corner_rows.append(jnp.where(k2 >= 2, last, 0))
        table = jnp.concatenate(picks, axis=0)

        def place(p, s):
            return s * side + p + flips[s] * (last - 2 * p)

        def corner_place(k):
            return SIDES * side + k * side + corner_rows[k]

        p = iota((side, 2 * SIDES * side), 0)
        r = iota((side, 2 * SIDES * side), 1)
        xs[1, t, 0:side, :] = dot(one_hot(r == place(p, 0)), table)
        xs[1, t, (ext - 1) * side :, :] = dot(one_hot(r == place(p, 2)), table)
        xs[1, t, side : (ext - 1) * side, :] = x_ref[t].astype(F32)
        half = ext // 2 * side

        def shift_rows(h, _, t=t):
            start = pl.multiple_of(h * half, side)
            rows = xs[1, t, pl.ds(start, half), :]
            cell = start + iota((half, 1), 0)
            i = cell // side - 1
            j = cell % side
            rr = iota((half, 2 * SIDES * side), 1)

            def column(sd, k_top, k_bottom):
                return jnp.where(
                    i < 0,
                    corner_place(k_top),
                    jnp.where(i > last, corner_place(k_bottom), place(i, sd)),
                )

            left = jnp.where(j == 0, column(3, 0, 3), -1)
            right = jnp.where(j == last, column(1, 1, 2), -1)
            ins_left = dot(one_hot(rr == left), table)
            ins_right = dot(one_hot(rr == right), table)
            xs[0, t, pl.ds(start, half), :] = jnp.where(j == 0, ins_left, pltpu.roll(rows, 1, 0))
            xs[2, t, pl.ds(start, half), :] = jnp.where(
                j == last, ins_right, pltpu.roll(rows, half - 1, 0)
            )
            return 0

        lax.fori_loop(0, 2, shift_rows, 0)
        gm_buf[t, 0:side, :] = jnp.zeros((side, channels), F32)
        gm_buf[t, (ext - 1) * side :, :] = jnp.zeros((side, channels), F32)

    chunks = side // chunk_rows

    def fold(v):
        return jnp.sum(v.reshape(v.shape[0] // 8, 8, v.shape[1]), axis=0)

    def step(idx, _):
        t = idx // chunks
        base = pl.multiple_of(lax.rem(idx, chunks) * n, n)
        mixed = jnp.zeros((n, channels), F32)
        for a in range(3):
            for b in range(3):
                w = dw_ref[3 * a + b : 3 * a + b + 1, :]
                mixed = mixed + xs[b, t, pl.ds(base + a * side, n), :] * w
        mean = jnp.mean(mixed, axis=-1, keepdims=True)
        centred = mixed - mean
        inv_std = lax.rsqrt(jnp.mean(centred * centred, axis=-1, keepdims=True) + 1e-06)
        unit = centred * inv_std
        normed = (unit * gain).astype(BF16)
        g = g_ref[t, pl.ds(base, n), :].astype(F32)
        mix = (g * scale).astype(BF16)
        branch = jnp.zeros((n, channels), F32)
        gn = jnp.zeros((n, channels), F32)
        for h in range(hidden // hb):
            cols = slice(h * hb, (h + 1) * hb)
            pre = dot(normed, w_in_ref[:, cols]) + bias_ref[:, cols]
            phi_cum = 0.5 * (1.0 + lax.erf(pre * INV_ROOT_TWO))
            act = (pre * phi_cum).astype(BF16)
            slope = phi_cum + pre * jnp.exp(-0.5 * pre * pre) * INV_ROOT_TAU
            gact = dot(mix, w_out_ref[cols, :], NT)
            ghf = (gact * slope).astype(BF16)
            branch = branch + dot(act, w_out_ref[cols, :])
            gn = gn + dot(ghf, w_in_ref[:, cols], NT)
            bias_acc[:, cols] += fold(ghf.astype(F32))
            gwi = dot(normed, ghf, TN)
            gwo = dot(mix, act, TN)
            for q in range(hb // lanes):
                blk = h * (hb // lanes) + q
                acc_ref[blk] += gwi[:, q * lanes : (q + 1) * lanes]
                acc_ref[hidden // lanes + blk] += gwo[:, q * lanes : (q + 1) * lanes]
        x = x_ref[t, pl.ds(base, n), :].astype(F32)
        out_ref[t, pl.ds(base, n), :] = (x + scale * branch).astype(BF16)
        vec_acc[0] += fold(gn * unit)
        vec_acc[1] += fold(g * branch)
        u = gn * gain
        gm = (
            u
            - jnp.mean(u, axis=-1, keepdims=True)
            - unit * jnp.mean(u * unit, axis=-1, keepdims=True)
        ) * inv_std
        gm_buf[t, pl.ds(base + side, n), :] = gm
        for a in range(3):
            for b in range(3):
                dw_acc[3 * a + b] += fold(gm * xs[b, t, pl.ds(base + a * side, n), :])
        return 0

    lax.fori_loop(0, tiles * chunks, step, 0)

    def taps(t, start, size, b):
        total = jnp.zeros((size, channels), F32)
        for a in range(3):
            w = dw_ref[3 * a + b : 3 * a + b + 1, :]
            total = total + gm_buf[t, pl.ds(start + (2 - a) * side, size), :] * w
        return total

    def back_step(idx, _):
        t = idx // chunks
        c = lax.rem(idx, chunks)
        base = pl.multiple_of(c * n, n)
        j = iota((n, 1), 0) % side
        left = taps(t, base, n, 0)
        right = taps(t, base, n, 2)
        grad = g_ref[t, pl.ds(base, n), :].astype(F32) + taps(t, base, n, 1)
        grad = grad + jnp.where(j == last, 0.0, pltpu.roll(left, n - 1, 0))
        grad = grad + jnp.where(j == 0, 0.0, pltpu.roll(right, 1, 0))
        xg_ref[t, pl.ds(base, n), :] = grad
        ri = iota((chunk_rows, n), 0)
        ci = iota((chunk_rows, n), 1)
        row0 = pl.multiple_of(c * chunk_rows, chunk_rows)
        strip_buf[t, pl.ds(3 * side + row0, chunk_rows), :] = dot(
            one_hot(ci == ri * side), left.astype(BF16)
        )
        strip_buf[t, pl.ds(side + row0, chunk_rows), :] = dot(
            one_hot(ci == ri * side + last), right.astype(BF16)
        )
        return 0

    lax.fori_loop(0, tiles * chunks, back_step, 0)
    j = iota((side, 1), 0)
    for t in range(tiles):
        for s, a, row in ((0, 0, 1), (2, 2, side)):
            edge = gm_buf[t, row * side : (row + 1) * side, :]
            left = edge * dw_ref[3 * a : 3 * a + 1, :]
            mid = edge * dw_ref[3 * a + 1 : 3 * a + 2, :]
            right = edge * dw_ref[3 * a + 2 : 3 * a + 3, :]
            mid = mid + jnp.where(j == last, 0.0, pltpu.roll(left, side - 1, 0))
            mid = mid + jnp.where(j == 0, 0.0, pltpu.roll(right, 1, 0))
            strip_buf[t, s * side : (s + 1) * side, :] = mid
            k_left, k_right = (0, 1) if s == 0 else (3, 2)
            at = SIDES * side
            strip_buf[t, at + k_left : at + k_left + 1, :] = left[0:1, :]
            strip_buf[t, at + k_right : at + k_right + 1, :] = right[last : last + 1, :]
    back_ref[...] = strip_buf[...].astype(BF16)
    for k in range(9):
        small_ref[k : k + 1, :] = jnp.sum(dw_acc[k], axis=0, keepdims=True)
    for k in range(2):
        small_ref[9 + k : 10 + k, :] = jnp.sum(vec_acc[k], axis=0, keepdims=True)
    for k in range(hidden // channels):
        small_ref[11 + k : 12 + k, :] = jnp.sum(
            bias_acc[:, k * channels : (k + 1) * channels], axis=0, keepdims=True
        )


def compute(seam, corner, strips, x, g, dw, gain, w_in, bias, w_out, scale):
    tiles, cells, channels = x.shape
    side = math.isqrt(cells)
    hidden = w_in.shape[1]
    ext = side + 2
    return pl.pallas_call(
        functools.partial(compute_kernel, side, tiles),
        out_shape=(
            jax.ShapeDtypeStruct(x.shape, BF16),
            jax.ShapeDtypeStruct(x.shape, F32),
            jax.ShapeDtypeStruct((tiles, SIDES * side + CORNER_ROWS, channels), BF16),
            jax.ShapeDtypeStruct((2 * hidden // 128, channels, 128), F32),
            jax.ShapeDtypeStruct((16, channels), F32),
        ),
        in_specs=[SMEM, SMEM] + [VMEM] * 9,
        out_specs=(VMEM,) * 5,
        scratch_shapes=[
            pltpu.VMEM((3, tiles, ext * side, channels), F32),
            pltpu.VMEM((tiles, ext * side, channels), F32),
            pltpu.VMEM((tiles, SIDES * side + CORNER_ROWS, channels), F32),
            pltpu.VMEM((9, 8, channels), F32),
            pltpu.VMEM((2, 8, channels), F32),
            pltpu.VMEM((8, hidden), F32),
        ],
        compiler_params=pltpu.CompilerParams(vmem_limit_bytes=50 * 2**20),
        name="block_grads",
    )(seam, corner, strips, x, g, dw, gain, w_in, bias, w_out, scale)


def digits_of(tile_size, rep_size):
    low = 2 ** (int(math.log2(rep_size)) // 2)
    core = ("tile", 1, 2)
    rest = ("tile", 2, tile_size // 2)
    near = ("rep", 1, low)
    far = ("rep", low, rep_size // low)
    return core, rest, near, far


def finish_kernel(
    side,
    tiles,
    factor,
    orders,
    seam_ref,
    corner_ref,
    back_ref,
    acc_ref,
    small_ref,
    table_ref,
    gwi_ref,
    gwo_ref,
    tot_ref,
    land,
    cur,
    snd,
    rcv,
    full,
    small_slots,
    halo_send,
    halo_recv,
    rs_send,
    rs_recv,
    ag_send,
    ag_recv,
    sm_send,
    sm_recv,
):
    tile_size = lax.axis_size("tile")
    rep_size = lax.axis_size("rep")
    index = {"tile": lax.axis_index("tile"), "rep": lax.axis_index("rep")}
    core, rest, near, far = digits_of(tile_size, rep_size)
    pieces = acc_ref.shape[0]
    part_size = pieces // len(orders)
    last = side - 1

    def digit(d):
        axis, stride, size = d
        return lax.rem(index[axis] // stride, size)

    def peer(d, value):
        axis, stride, size = d
        return {axis: index[axis] + (value - digit(d)) * stride}

    barrier = pltpu.get_barrier_semaphore()
    signals = 0
    for k in range(1, tile_size):
        pl.semaphore_signal(
            barrier,
            inc=1,
            device_id={"tile": lax.rem(index["tile"] + k, tile_size)},
            device_id_type=MESH,
        )
        signals += 1
    for d in (near, far):
        for k in range(1, d[2]):
            pl.semaphore_signal(
                barrier,
                inc=1,
                device_id=peer(d, lax.rem(digit(d) + k, d[2])),
                device_id_type=MESH,
            )
            signals += 1
    pl.semaphore_wait(barrier, signals)

    land[pl.ds(index["tile"] * tiles, tiles)] = back_ref[...]

    offsets = []
    for part, order in enumerate(orders):
        off = part * part_size
        size = part_size
        stages = []
        for d in order:
            size = size // d[2]
            stages.append((off, size))
            off = off + digit(d) * size
        stages.append((off, size))
        offsets.append(stages)
    sem_at = {}
    rcv_at = {}
    sems = 0
    rows = 0
    for part, order in enumerate(orders):
        for s, d in enumerate(order):
            sem_at[part, s] = sems
            rcv_at[part, s] = rows
            sems += d[2] - 1
            rows += (d[2] - 1) * offsets[part][s][1]

    def start_scatter(part, s):
        d = orders[part][s]
        off, size = offsets[part][s]
        src = acc_ref if s == 0 else cur
        copies = []
        for k in range(1, d[2]):
            to = lax.rem(digit(d) + k, d[2])
            where = pl.ds(off + to * size, size)
            snd[where] = src[where].astype(BF16)
            copy = pltpu.make_async_remote_copy(
                src_ref=snd.at[where],
                dst_ref=rcv.at[pl.ds(rcv_at[part, s] + (k - 1) * size, size)],
                send_sem=rs_send.at[sem_at[part, s] + k - 1],
                recv_sem=rs_recv.at[sem_at[part, s] + k - 1],
                device_id=peer(d, to),
                device_id_type=MESH,
            )
            copy.start()
            copies.append(copy)
        return copies

    def end_scatter(part, s, copies):
        d = orders[part][s]
        _, size = offsets[part][s]
        off, _ = offsets[part][s + 1]
        src = acc_ref if s == 0 else cur
        total = src[pl.ds(off, size)]
        for k, copy in enumerate(copies):
            copy.wait_recv()
            total = total + rcv[pl.ds(rcv_at[part, s] + k * size, size)].astype(F32)
        if s == len(orders[part]) - 1:
            full[pl.ds(off, size)] = (total * factor).astype(BF16)
        else:
            cur[pl.ds(off, size)] = total

    def start_gather(part, s):
        d = orders[part][s]
        off, size = offsets[part][s + 1][0], offsets[part][s][1]
        copies = []
        for k in range(1, d[2]):
            to = lax.rem(digit(d) + k, d[2])
            copy = pltpu.make_async_remote_copy(
                src_ref=full.at[pl.ds(off, size)],
                dst_ref=full.at[pl.ds(off, size)],
                send_sem=ag_send.at[sem_at[part, s] + k - 1],
                recv_sem=ag_recv.at[sem_at[part, s] + k - 1],
                device_id=peer(d, to),
                device_id_type=MESH,
            )
            copy.start()
            copies.append(copy)
        return copies

    small_order = orders[0]
    small_base = [0]
    small_sem = [0]
    for d in small_order:
        small_base.append(small_base[-1] + d[2])
        small_sem.append(small_sem[-1] + d[2] - 1)

    def start_small(s, value):
        d = small_order[s]
        mine = small_base[s] + digit(d)
        small_slots[mine] = value
        copies = []
        for k in range(1, d[2]):
            to = lax.rem(digit(d) + k, d[2])
            copy = pltpu.make_async_remote_copy(
                src_ref=small_slots.at[mine],
                dst_ref=small_slots.at[mine],
                send_sem=sm_send.at[small_sem[s] + k - 1],
                recv_sem=sm_recv.at[small_sem[s] + k - 1],
                device_id=peer(d, to),
                device_id_type=MESH,
            )
            copy.start()
            copies.append(copy)
        return copies

    def end_small(s, copies):
        for copy in copies:
            copy.wait_recv()
        total = small_slots[small_base[s]]
        for k in range(1, small_order[s][2]):
            total = total + small_slots[small_base[s] + k]
        return total

    every = []
    stage_count = len(small_order)
    part_ids = range(len(orders))
    flying = {}
    for part in part_ids:
        flying[part] = start_scatter(part, 0)
        every += flying[part]
    refs = (tiles, land, halo_send, halo_recv)
    halo = tile_gather(*refs)
    small = start_small(0, small_ref[...])
    every += small
    for s in range(stage_count):
        for part in part_ids:
            end_scatter(part, s, flying[part])
            if s + 1 < stage_count:
                flying[part] = start_scatter(part, s + 1)
            else:
                flying[part] = start_gather(part, s)
            every += flying[part]
        if s == 0:
            halo = tile_forward(halo, *refs)
        value = end_small(s, small)
        if s + 1 < stage_count:
            small = start_small(s + 1, value)
            every += small
    tot_ref[...] = value * factor

    def return_halos():
        tile_end(*halo)
        width = SIDES * side + CORNER_ROWS
        total_rows = land.shape[0] * width
        home = land[...].reshape(total_rows, land.shape[2])
        row = iota((width, 1), 0)
        rr = iota((width, total_rows), 1)
        for t in range(tiles):
            source = jnp.full((width, 1), -1, jnp.int32)
            for s in range(SIDES):
                t2, s2, f = seam_ref[t, s, 0], seam_ref[t, s, 1], seam_ref[t, s, 2]
                flip = f + (1 if s >= 2 else 0) + s2 // 2
                flip = flip - 2 * (flip // 2)
                p = row - s * side
                at = t2 * width + s2 * side + p + flip * (last - 2 * p)
                source = jnp.where((row >= s * side) & (row < (s + 1) * side), at, source)
            for k in range(4):
                t2, k2 = corner_ref[t, k, 0], corner_ref[t, k, 1]
                at = t2 * width + SIDES * side + k2
                source = jnp.where(row == SIDES * side + k, at, source)
            table_ref[t] = dot(one_hot(rr == source), home).astype(BF16)

    for s in reversed(range(stage_count)):
        for part in part_ids:
            for copy in flying[part]:
                copy.wait_recv()
            if s > 0:
                flying[part] = start_gather(part, s - 1)
                every += flying[part]
        if s == 1:
            return_halos()
    channels = gwi_ref.shape[0]
    hidden = gwi_ref.shape[1]
    per = channels // 16
    for h in range(hidden // 128):
        block = full[pl.ds(h * per, per)].astype(F32).reshape(channels, 128)
        gwi_ref[:, h * 128 : (h + 1) * 128] = block
        at = (hidden // 128 + h) * per
        block = full[pl.ds(at, per)].astype(F32).reshape(channels, 128)
        gwo_ref[h * 128 : (h + 1) * 128, :] = block.T
    for copy in every:
        copy.wait_send()


def finish(seam, corner, side, back, acc, small, factor):
    tiles, _, channels = back.shape
    tile_size = lax.axis_size("tile")
    rep_size = lax.axis_size("rep")
    acc = acc.reshape(-1, 16, 128)
    hidden = acc.shape[0] * 16 * 128 // (2 * channels)
    core, rest, near, far = digits_of(tile_size, rep_size)
    orders = [(core, rest, near, far), (core, near, rest, far)]
    if acc.shape[0] < 4 * tile_size * rep_size:
        orders = orders[:1]
    else:
        orders = orders * 2
    sems = 0
    rows = 0
    for order in orders:
        size = acc.shape[0] // len(orders)
        for d in order:
            size = size // d[2]
            sems += d[2] - 1
            rows += (d[2] - 1) * size
    slots = sum(d[2] for d in orders[0])
    dma = pltpu.SemaphoreType.DMA
    return pl.pallas_call(
        functools.partial(finish_kernel, side, tiles, factor, orders),
        out_shape=(
            jax.ShapeDtypeStruct(back.shape, BF16),
            jax.ShapeDtypeStruct((channels, hidden), F32),
            jax.ShapeDtypeStruct((hidden, channels), F32),
            jax.ShapeDtypeStruct(small.shape, F32),
        ),
        in_specs=[SMEM, SMEM] + [VMEM] * 3,
        out_specs=(VMEM,) * 4,
        scratch_shapes=[
            pltpu.VMEM((tile_size * tiles,) + back.shape[1:], BF16),
            pltpu.VMEM(acc.shape, F32),
            pltpu.VMEM(acc.shape, BF16),
            pltpu.VMEM((rows, 16, 128), BF16),
            pltpu.VMEM(acc.shape, BF16),
            pltpu.VMEM((slots,) + small.shape, F32),
            dma((tile_size - 1,)),
            dma((tile_size - 1,)),
            dma((sems,)),
            dma((sems,)),
            dma((sems,)),
            dma((sems,)),
            dma((slots,)),
            dma((slots,)),
        ],
        compiler_params=pltpu.CompilerParams(
            collective_id=1, has_side_effects=True, vmem_limit_bytes=50 * 2**20
        ),
        name="grad_sum",
    )(seam, corner, back, acc, small)


def rim_kernel(side, table_ref, xg_in, xg_ref):
    last = side - 1
    cells = side * side
    width = table_ref.shape[1]
    cell = iota((cells, 1), 0)
    i = cell // side
    j = cell % side
    r = iota((cells, width), 1)
    rim = None
    for s, (on, p) in enumerate(((i == 0, j), (j == last, i), (i == last, j), (j == 0, i))):
        hit = r == jnp.where(on, s * side + p, -1)
        rim = hit if rim is None else rim | hit
    for k, cell_k in enumerate((0, last, cells - 1, cells - side)):
        rim = rim | (r == jnp.where(cell == cell_k, SIDES * side + k, -1))
    rim = one_hot(rim)
    xg_ref[0] = xg_in[0] + dot(rim, table_ref[0])


def add_rims(xg, table):
    tiles, cells, channels = xg.shape
    block = pl.BlockSpec((1, cells, channels), lambda t: (t, 0, 0))
    return pl.pallas_call(
        functools.partial(rim_kernel, math.isqrt(cells)),
        grid=(tiles,),
        out_shape=jax.ShapeDtypeStruct(xg.shape, F32),
        in_specs=[pl.BlockSpec((1,) + table.shape[1:], lambda t: (t, 0, 0)), block],
        out_specs=block,
        compiler_params=pltpu.CompilerParams(vmem_limit_bytes=32 * 2**20),
        name="add_rims",
    )(table, xg)


def body(
    inputs,
    grad_out,
    seam_links,
    corner_links,
    dw_weight,
    norm_gain,
    w_in,
    bias_in,
    w_out,
    layer_scale,
):
    samples, local, side, _, channels = inputs.shape
    tiles = samples * local
    x = inputs.reshape(tiles, side * side, channels)
    g = grad_out.reshape(tiles, side * side, channels)
    cell_total = lax.axis_size("tile") * lax.axis_size("rep") * tiles * side * side
    factor = 1.0 / math.sqrt(cell_total)
    strips = gather_halos(x)
    out, xg, back, acc, small = compute(
        seam_links,
        corner_links,
        strips,
        x,
        g,
        dw_weight.T,
        norm_gain[None],
        w_in,
        bias_in[None],
        w_out,
        layer_scale[None],
    )
    table, gwi, gwo, total = finish(seam_links, corner_links, side, back, acc, small, factor)
    xg = add_rims(xg, table)
    return (
        out.reshape(inputs.shape),
        xg.reshape(inputs.shape),
        total[0:9].T,
        total[9],
        gwi,
        total[11 : 11 + w_in.shape[1] // channels].reshape(-1),
        gwo,
        total[10],
    )


def solution(mesh):
    placed = (
        P("rep", "tile", None, None, None),
        P("rep", "tile", None, None, None),
        P("tile", None, None),
        P("tile", None, None),
        P(),
        P(),
        P(),
        P(),
        P(),
        P(),
    )
    return jax.shard_map(
        body,
        mesh=mesh,
        in_specs=placed,
        out_specs=(
            P("rep", "tile", None, None, None),
            P("rep", "tile", None, None, None),
            P(),
            P(),
            P(),
            P(),
            P(),
            P(),
        ),
        check_vma=False,
    )
```

```python
import functools
import math

import jax
import jax.numpy as jnp
from jax import lax
from jax.experimental import pallas as pl
from jax.experimental.pallas import tpu as pltpu
from jax.sharding import PartitionSpec as P

INV_ROOT_TWO = 0.7071067811865476
INV_ROOT_TAU = 0.3989422804014327
MESH = pl.DeviceIdType.MESH
F32 = jnp.float32
BF16 = jnp.bfloat16
VMEM = pl.BlockSpec(memory_space=pltpu.VMEM)
SMEM = pl.BlockSpec(memory_space=pltpu.SMEM)
NN = (((1,), (0,)), ((), ()))
NT = (((1,), (1,)), ((), ()))
TN = (((0,), (0,)), ((), ()))
SIDES = 4
CORNER_ROWS = 16


def dot(a, b, dims=NN):
    return lax.dot_general(a, b, dims, preferred_element_type=F32)


def iota(shape, dim):
    return lax.broadcasted_iota(jnp.int32, shape, dim)


def one_hot(mask):
    return jnp.where(mask, 1.0, 0.0).astype(BF16)


def block_copy(tiles, buf, send_sem, recv_sem, block, to, slot):
    where = pl.ds(block * tiles, tiles)
    copy = pltpu.make_async_remote_copy(
        src_ref=buf.at[where],
        dst_ref=buf.at[where],
        send_sem=send_sem.at[slot],
        recv_sem=recv_sem.at[slot],
        device_id={"tile": to},
        device_id_type=MESH,
    )
    copy.start()
    return copy


def tile_gather(*refs):
    size = lax.axis_size("tile")
    me = lax.axis_index("tile")
    far = [
        block_copy(*refs, me, lax.rem(me + 2 * k, size), k - 1) for k in range(1, size // 2)
    ]
    near = block_copy(*refs, me, me + 1 - 2 * lax.rem(me, 2), size // 2 - 1)
    return far, near


def tile_forward(started, *refs):
    size = lax.axis_size("tile")
    me = lax.axis_index("tile")
    far, near = started
    passed = []
    for k, copy in enumerate(far, 1):
        copy.wait_recv()
        block = lax.rem(me + size - 2 * k, size)
        passed.append(
            block_copy(*refs, block, me + 1 - 2 * lax.rem(me, 2), size // 2 - 1 + k)
        )
    return far, [near] + passed


def tile_end(far, near):
    for copy in near:
        copy.wait_recv()
    for copy in far + near:
        copy.wait_send()


def halo_kernel(side, tiles, x_ref, out_ref, land, send_sem, recv_sem):
    size = lax.axis_size("tile")
    me = lax.axis_index("tile")
    barrier = pltpu.get_barrier_semaphore()
    for k in range(1, size):
        pl.semaphore_signal(
            barrier, inc=1, device_id={"tile": lax.rem(me + k, size)}, device_id_type=MESH
        )
    rows = SIDES * side
    cells = side * side
    r = iota((rows, cells), 0)
    c = iota((rows, cells), 1)
    s = r // side
    p = r % side
    target = jnp.where(
        s == 0,
        p,
        jnp.where(
            s == 1,
            p * side + side - 1,
            jnp.where(s == 2, (side - 1) * side + p, p * side),
        ),
    )
    sel = one_hot(c == target)
    for t in range(tiles):
        land[me * tiles + t] = dot(sel, x_ref[t]).astype(BF16)
    pl.semaphore_wait(barrier, size - 1)
    refs = (tiles, land, send_sem, recv_sem)
    tile_end(*tile_forward(tile_gather(*refs), *refs))
    out_ref[...] = land[...]


def gather_halos(x):
    tiles, cells, channels = x.shape
    side = math.isqrt(cells)
    size = lax.axis_size("tile")
    shape = (size * tiles, SIDES * side, channels)
    return pl.pallas_call(
        functools.partial(halo_kernel, side, tiles),
        out_shape=jax.ShapeDtypeStruct(shape, BF16),
        in_specs=[VMEM],
        out_specs=VMEM,
        scratch_shapes=[
            pltpu.VMEM(shape, BF16),
            pltpu.SemaphoreType.DMA((size - 1,)),
            pltpu.SemaphoreType.DMA((size - 1,)),
        ],
        compiler_params=pltpu.CompilerParams(
            collective_id=0, has_side_effects=True, vmem_limit_bytes=60 * 2**20
        ),
        name="halo_gather",
    )(x)


def compute_kernel(
    side,
    tiles,
    seam_ref,
    corner_ref,
    strips_ref,
    x_ref,
    g_ref,
    dw_ref,
    gain_ref,
    w_in_ref,
    bias_ref,
    w_out_ref,
    scale_ref,
    out_ref,
    xg_ref,
    back_ref,
    acc_ref,
    small_ref,
    xs,
    gm_buf,
    strip_buf,
    dw_acc,
    vec_acc,
    bias_acc,
):
    channels = x_ref.shape[-1]
    hidden = w_in_ref.shape[1]
    ext = side + 2
    last = side - 1
    gain = gain_ref[...]
    scale = scale_ref[...]
    chunk_rows = 8
    n = chunk_rows * side
    hb = 256
    lanes = 128

    dw_acc[...] = jnp.zeros_like(dw_acc)
    vec_acc[...] = jnp.zeros_like(vec_acc)
    bias_acc[...] = jnp.zeros_like(bias_acc)
    acc_ref[...] = jnp.zeros_like(acc_ref)
    small_ref[...] = jnp.zeros_like(small_ref)
    strip_buf[...] = jnp.zeros_like(strip_buf)

    for t in range(tiles):
        picks = []
        flips = []
        for s in range(SIDES):
            t2, s2, f = seam_ref[t, s, 0], seam_ref[t, s, 1], seam_ref[t, s, 2]
            flip = lax.rem(f + (1 if s >= 2 else 0) + jnp.where(s2 >= 2, 1, 0), 2)
            picks.append(strips_ref[t2, pl.ds(pl.multiple_of(s2 * side, side), side), :])
            flips.append(flip)
        corner_rows = []
        for k in range(4):
            t2, k2 = corner_ref[t, k, 0], corner_ref[t, k, 1]
            picks.append(strips_ref[t2, pl.ds(pl.multiple_of(k2 * side, side), side), :])
            corner_rows.append(jnp.where(k2 >= 2, last, 0))
        table = jnp.concatenate(picks, axis=0)

        def place(p, s):
            return s * side + p + flips[s] * (last - 2 * p)

        def corner_place(k):
            return SIDES * side + k * side + corner_rows[k]

        p = iota((side, 2 * SIDES * side), 0)
        r = iota((side, 2 * SIDES * side), 1)
        xs[1, t, 0:side, :] = dot(one_hot(r == place(p, 0)), table)
        xs[1, t, (ext - 1) * side :, :] = dot(one_hot(r == place(p, 2)), table)
        xs[1, t, side : (ext - 1) * side, :] = x_ref[t].astype(F32)
        half = ext // 2 * side

        def shift_rows(h, _, t=t):
            start = pl.multiple_of(h * half, side)
            rows = xs[1, t, pl.ds(start, half), :]
            cell = start + iota((half, 1), 0)
            i = cell // side - 1
            j = cell % side
            rr = iota((half, 2 * SIDES * side), 1)

            def column(sd, k_top, k_bottom):
                return jnp.where(
                    i < 0,
                    corner_place(k_top),
                    jnp.where(i > last, corner_place(k_bottom), place(i, sd)),
                )

            left = jnp.where(j == 0, column(3, 0, 3), -1)
            right = jnp.where(j == last, column(1, 1, 2), -1)
            ins_left = dot(one_hot(rr == left), table)
            ins_right = dot(one_hot(rr == right), table)
            xs[0, t, pl.ds(start, half), :] = jnp.where(j == 0, ins_left, pltpu.roll(rows, 1, 0))
            xs[2, t, pl.ds(start, half), :] = jnp.where(
                j == last, ins_right, pltpu.roll(rows, half - 1, 0)
            )
            return 0

        lax.fori_loop(0, 2, shift_rows, 0)
        gm_buf[t, 0:side, :] = jnp.zeros((side, channels), F32)
        gm_buf[t, (ext - 1) * side :, :] = jnp.zeros((side, channels), F32)

    chunks = side // chunk_rows

    def fold(v):
        return jnp.sum(v.reshape(v.shape[0] // 8, 8, v.shape[1]), axis=0)

    def step(idx, _):
        t = idx // chunks
        base = pl.multiple_of(lax.rem(idx, chunks) * n, n)
        mixed = jnp.zeros((n, channels), F32)
        for a in range(3):
            for b in range(3):
                w = dw_ref[3 * a + b : 3 * a + b + 1, :]
                mixed = mixed + xs[b, t, pl.ds(base + a * side, n), :] * w
        mean = jnp.mean(mixed, axis=-1, keepdims=True)
        centred = mixed - mean
        inv_std = lax.rsqrt(jnp.mean(centred * centred, axis=-1, keepdims=True) + 1e-06)
        unit = centred * inv_std
        normed = (unit * gain).astype(BF16)
        g = g_ref[t, pl.ds(base, n), :].astype(F32)
        mix = (g * scale).astype(BF16)
        branch = jnp.zeros((n, channels), F32)
        gn = jnp.zeros((n, channels), F32)
        for h in range(hidden // hb):
            cols = slice(h * hb, (h + 1) * hb)
            pre = dot(normed, w_in_ref[:, cols]) + bias_ref[:, cols]
            phi_cum = 0.5 * (1.0 + lax.erf(pre * INV_ROOT_TWO))
            act = (pre * phi_cum).astype(BF16)
            slope = phi_cum + pre * jnp.exp(-0.5 * pre * pre) * INV_ROOT_TAU
            gact = dot(mix, w_out_ref[cols, :], NT)
            ghf = (gact * slope).astype(BF16)
            branch = branch + dot(act, w_out_ref[cols, :])
            gn = gn + dot(ghf, w_in_ref[:, cols], NT)
            bias_acc[:, cols] += fold(ghf.astype(F32))
            gwi = dot(normed, ghf, TN)
            gwo = dot(mix, act, TN)
            for q in range(hb // lanes):
                blk = h * (hb // lanes) + q
                acc_ref[blk] += gwi[:, q * lanes : (q + 1) * lanes]
                acc_ref[hidden // lanes + blk] += gwo[:, q * lanes : (q + 1) * lanes]
        x = x_ref[t, pl.ds(base, n), :].astype(F32)
        out_ref[t, pl.ds(base, n), :] = (x + scale * branch).astype(BF16)
        vec_acc[0] += fold(gn * unit)
        vec_acc[1] += fold(g * branch)
        u = gn * gain
        gm = (
            u
            - jnp.mean(u, axis=-1, keepdims=True)
            - unit * jnp.mean(u * unit, axis=-1, keepdims=True)
        ) * inv_std
        gm_buf[t, pl.ds(base + side, n), :] = gm
        for a in range(3):
            for b in range(3):
                dw_acc[3 * a + b] += fold(gm * xs[b, t, pl.ds(base + a * side, n), :])
        return 0

    lax.fori_loop(0, tiles * chunks, step, 0)

    def taps(t, start, size, b):
        total = jnp.zeros((size, channels), F32)
        for a in range(3):
            w = dw_ref[3 * a + b : 3 * a + b + 1, :]
            total = total + gm_buf[t, pl.ds(start + (2 - a) * side, size), :] * w
        return total

    def back_step(idx, _):
        t = idx // chunks
        c = lax.rem(idx, chunks)
        base = pl.multiple_of(c * n, n)
        j = iota((n, 1), 0) % side
        left = taps(t, base, n, 0)
        right = taps(t, base, n, 2)
        grad = g_ref[t, pl.ds(base, n), :].astype(F32) + taps(t, base, n, 1)
        grad = grad + jnp.where(j == last, 0.0, pltpu.roll(left, n - 1, 0))
        grad = grad + jnp.where(j == 0, 0.0, pltpu.roll(right, 1, 0))
        xg_ref[t, pl.ds(base, n), :] = grad
        ri = iota((chunk_rows, n), 0)
        ci = iota((chunk_rows, n), 1)
        row0 = pl.multiple_of(c * chunk_rows, chunk_rows)
        strip_buf[t, pl.ds(3 * side + row0, chunk_rows), :] = dot(
            one_hot(ci == ri * side), left.astype(BF16)
        )
        strip_buf[t, pl.ds(side + row0, chunk_rows), :] = dot(
            one_hot(ci == ri * side + last), right.astype(BF16)
        )
        return 0

    lax.fori_loop(0, tiles * chunks, back_step, 0)
    j = iota((side, 1), 0)
    for t in range(tiles):
        for s, a, row in ((0, 0, 1), (2, 2, side)):
            edge = gm_buf[t, row * side : (row + 1) * side, :]
            left = edge * dw_ref[3 * a : 3 * a + 1, :]
            mid = edge * dw_ref[3 * a + 1 : 3 * a + 2, :]
            right = edge * dw_ref[3 * a + 2 : 3 * a + 3, :]
            mid = mid + jnp.where(j == last, 0.0, pltpu.roll(left, side - 1, 0))
            mid = mid + jnp.where(j == 0, 0.0, pltpu.roll(right, 1, 0))
            strip_buf[t, s * side : (s + 1) * side, :] = mid
            k_left, k_right = (0, 1) if s == 0 else (3, 2)
            at = SIDES * side
            strip_buf[t, at + k_left : at + k_left + 1, :] = left[0:1, :]
            strip_buf[t, at + k_right : at + k_right + 1, :] = right[last : last + 1, :]
    back_ref[...] = strip_buf[...].astype(BF16)
    for k in range(9):
        small_ref[k : k + 1, :] = jnp.sum(dw_acc[k], axis=0, keepdims=True)
    for k in range(2):
        small_ref[9 + k : 10 + k, :] = jnp.sum(vec_acc[k], axis=0, keepdims=True)
    for k in range(hidden // channels):
        small_ref[11 + k : 12 + k, :] = jnp.sum(
            bias_acc[:, k * channels : (k + 1) * channels], axis=0, keepdims=True
        )


def compute(seam, corner, strips, x, g, dw, gain, w_in, bias, w_out, scale):
    tiles, cells, channels = x.shape
    side = math.isqrt(cells)
    hidden = w_in.shape[1]
    ext = side + 2
    return pl.pallas_call(
        functools.partial(compute_kernel, side, tiles),
        out_shape=(
            jax.ShapeDtypeStruct(x.shape, BF16),
            jax.ShapeDtypeStruct(x.shape, F32),
            jax.ShapeDtypeStruct((tiles, SIDES * side + CORNER_ROWS, channels), BF16),
            jax.ShapeDtypeStruct((2 * hidden // 128, channels, 128), F32),
            jax.ShapeDtypeStruct((16, channels), F32),
        ),
        in_specs=[SMEM, SMEM] + [VMEM] * 9,
        out_specs=(VMEM,) * 5,
        scratch_shapes=[
            pltpu.VMEM((3, tiles, ext * side, channels), F32),
            pltpu.VMEM((tiles, ext * side, channels), F32),
            pltpu.VMEM((tiles, SIDES * side + CORNER_ROWS, channels), F32),
            pltpu.VMEM((9, 8, channels), F32),
            pltpu.VMEM((2, 8, channels), F32),
            pltpu.VMEM((8, hidden), F32),
        ],
        compiler_params=pltpu.CompilerParams(vmem_limit_bytes=60 * 2**20),
        name="block_grads",
    )(seam, corner, strips, x, g, dw, gain, w_in, bias, w_out, scale)


def digits_of(tile_size, rep_size):
    low = 2 ** (int(math.log2(rep_size)) // 2)
    core = ("tile", 1, 2)
    rest = ("tile", 2, tile_size // 2)
    near = ("rep", 1, low)
    far = ("rep", low, rep_size // low)
    return core, rest, near, far


def finish_kernel(
    side,
    tiles,
    factor,
    orders,
    seam_ref,
    corner_ref,
    back_ref,
    acc_ref,
    small_ref,
    table_ref,
    gwi_ref,
    gwo_ref,
    tot_ref,
    land,
    cur,
    snd,
    rcv,
    full,
    small_slots,
    halo_send,
    halo_recv,
    rs_send,
    rs_recv,
    ag_send,
    ag_recv,
    sm_send,
    sm_recv,
):
    tile_size = lax.axis_size("tile")
    rep_size = lax.axis_size("rep")
    index = {"tile": lax.axis_index("tile"), "rep": lax.axis_index("rep")}
    core, rest, near, far = digits_of(tile_size, rep_size)
    pieces = acc_ref.shape[0]
    part_size = pieces // len(orders)
    last = side - 1

    def digit(d):
        axis, stride, size = d
        return lax.rem(index[axis] // stride, size)

    def peer(d, value):
        axis, stride, size = d
        return {axis: index[axis] + (value - digit(d)) * stride}

    barrier = pltpu.get_barrier_semaphore()
    signals = 0
    for k in range(1, tile_size):
        pl.semaphore_signal(
            barrier,
            inc=1,
            device_id={"tile": lax.rem(index["tile"] + k, tile_size)},
            device_id_type=MESH,
        )
        signals += 1
    for d in (near, far):
        for k in range(1, d[2]):
            pl.semaphore_signal(
                barrier,
                inc=1,
                device_id=peer(d, lax.rem(digit(d) + k, d[2])),
                device_id_type=MESH,
            )
            signals += 1
    pl.semaphore_wait(barrier, signals)

    land[pl.ds(index["tile"] * tiles, tiles)] = back_ref[...]

    offsets = []
    for part, order in enumerate(orders):
        off = part * part_size
        size = part_size
        stages = []
        for d in order:
            size = size // d[2]
            stages.append((off, size))
            off = off + digit(d) * size
        stages.append((off, size))
        offsets.append(stages)
    sem_at = {}
    rcv_at = {}
    sems = 0
    rows = 0
    for part, order in enumerate(orders):
        for s, d in enumerate(order):
            sem_at[part, s] = sems
            rcv_at[part, s] = rows
            sems += d[2] - 1
            rows += (d[2] - 1) * offsets[part][s][1]

    def start_scatter(part, s):
        d = orders[part][s]
        off, size = offsets[part][s]
        src = acc_ref if s == 0 else cur
        copies = []
        for k in range(1, d[2]):
            to = lax.rem(digit(d) + k, d[2])
            where = pl.ds(off + to * size, size)
            snd[where] = src[where].astype(BF16)
            copy = pltpu.make_async_remote_copy(
                src_ref=snd.at[where],
                dst_ref=rcv.at[pl.ds(rcv_at[part, s] + (k - 1) * size, size)],
                send_sem=rs_send.at[sem_at[part, s] + k - 1],
                recv_sem=rs_recv.at[sem_at[part, s] + k - 1],
                device_id=peer(d, to),
                device_id_type=MESH,
            )
            copy.start()
            copies.append(copy)
        return copies

    def end_scatter(part, s, copies):
        d = orders[part][s]
        _, size = offsets[part][s]
        off, _ = offsets[part][s + 1]
        src = acc_ref if s == 0 else cur
        total = src[pl.ds(off, size)]
        for k, copy in enumerate(copies):
            copy.wait_recv()
            total = total + rcv[pl.ds(rcv_at[part, s] + k * size, size)].astype(F32)
        if s == len(orders[part]) - 1:
            full[pl.ds(off, size)] = (total * factor).astype(BF16)
        else:
            cur[pl.ds(off, size)] = total

    def start_gather(part, s):
        d = orders[part][s]
        off, size = offsets[part][s + 1][0], offsets[part][s][1]
        copies = []
        for k in range(1, d[2]):
            to = lax.rem(digit(d) + k, d[2])
            copy = pltpu.make_async_remote_copy(
                src_ref=full.at[pl.ds(off, size)],
                dst_ref=full.at[pl.ds(off, size)],
                send_sem=ag_send.at[sem_at[part, s] + k - 1],
                recv_sem=ag_recv.at[sem_at[part, s] + k - 1],
                device_id=peer(d, to),
                device_id_type=MESH,
            )
            copy.start()
            copies.append(copy)
        return copies

    small_order = orders[0]
    small_base = [0]
    small_sem = [0]
    for d in small_order:
        small_base.append(small_base[-1] + d[2])
        small_sem.append(small_sem[-1] + d[2] - 1)

    def start_small(s, value):
        d = small_order[s]
        mine = small_base[s] + digit(d)
        small_slots[mine] = value
        copies = []
        for k in range(1, d[2]):
            to = lax.rem(digit(d) + k, d[2])
            copy = pltpu.make_async_remote_copy(
                src_ref=small_slots.at[mine],
                dst_ref=small_slots.at[mine],
                send_sem=sm_send.at[small_sem[s] + k - 1],
                recv_sem=sm_recv.at[small_sem[s] + k - 1],
                device_id=peer(d, to),
                device_id_type=MESH,
            )
            copy.start()
            copies.append(copy)
        return copies

    def end_small(s, copies):
        for copy in copies:
            copy.wait_recv()
        total = small_slots[small_base[s]]
        for k in range(1, small_order[s][2]):
            total = total + small_slots[small_base[s] + k]
        return total

    every = []
    stage_count = len(small_order)
    part_ids = range(len(orders))
    flying = {}
    for part in part_ids:
        flying[part] = start_scatter(part, 0)
        every += flying[part]
    refs = (tiles, land, halo_send, halo_recv)
    halo = tile_gather(*refs)
    small = start_small(0, small_ref[...])
    every += small
    for s in range(stage_count):
        for part in part_ids:
            end_scatter(part, s, flying[part])
            if s + 1 < stage_count:
                flying[part] = start_scatter(part, s + 1)
            else:
                flying[part] = start_gather(part, s)
            every += flying[part]
        if s == 0:
            halo = tile_forward(halo, *refs)
        value = end_small(s, small)
        if s + 1 < stage_count:
            small = start_small(s + 1, value)
            every += small
    tot_ref[...] = value * factor

    def return_halos():
        tile_end(*halo)
        width = SIDES * side + CORNER_ROWS
        total_rows = land.shape[0] * width
        home = land[...].reshape(total_rows, land.shape[2])
        row = iota((width, 1), 0)
        rr = iota((width, total_rows), 1)
        for t in range(tiles):
            source = jnp.full((width, 1), -1, jnp.int32)
            for s in range(SIDES):
                t2, s2, f = seam_ref[t, s, 0], seam_ref[t, s, 1], seam_ref[t, s, 2]
                flip = f + (1 if s >= 2 else 0) + s2 // 2
                flip = flip - 2 * (flip // 2)
                p = row - s * side
                at = t2 * width + s2 * side + p + flip * (last - 2 * p)
                source = jnp.where((row >= s * side) & (row < (s + 1) * side), at, source)
            for k in range(4):
                t2, k2 = corner_ref[t, k, 0], corner_ref[t, k, 1]
                at = t2 * width + SIDES * side + k2
                source = jnp.where(row == SIDES * side + k, at, source)
            table_ref[t] = dot(one_hot(rr == source), home).astype(BF16)

    for s in reversed(range(stage_count)):
        for part in part_ids:
            for copy in flying[part]:
                copy.wait_recv()
            if s > 0:
                flying[part] = start_gather(part, s - 1)
                every += flying[part]
        if s == 1:
            return_halos()
    channels = gwi_ref.shape[0]
    hidden = gwi_ref.shape[1]
    per = channels // 16
    for h in range(hidden // 128):
        block = full[pl.ds(h * per, per)].astype(F32).reshape(channels, 128)
        gwi_ref[:, h * 128 : (h + 1) * 128] = block
        at = (hidden // 128 + h) * per
        block = full[pl.ds(at, per)].astype(F32).reshape(channels, 128)
        gwo_ref[h * 128 : (h + 1) * 128, :] = block.T
    for copy in every:
        copy.wait_send()


def finish(seam, corner, side, back, acc, small, factor):
    tiles, _, channels = back.shape
    tile_size = lax.axis_size("tile")
    rep_size = lax.axis_size("rep")
    acc = acc.reshape(-1, 16, 128)
    hidden = acc.shape[0] * 16 * 128 // (2 * channels)
    core, rest, near, far = digits_of(tile_size, rep_size)
    orders = [(core, rest, near, far), (core, near, rest, far)]
    if acc.shape[0] < 4 * tile_size * rep_size:
        orders = orders[:1]
    else:
        orders = orders * 2
    sems = 0
    rows = 0
    for order in orders:
        size = acc.shape[0] // len(orders)
        for d in order:
            size = size // d[2]
            sems += d[2] - 1
            rows += (d[2] - 1) * size
    slots = sum(d[2] for d in orders[0])
    dma = pltpu.SemaphoreType.DMA
    return pl.pallas_call(
        functools.partial(finish_kernel, side, tiles, factor, orders),
        out_shape=(
            jax.ShapeDtypeStruct(back.shape, BF16),
            jax.ShapeDtypeStruct((channels, hidden), F32),
            jax.ShapeDtypeStruct((hidden, channels), F32),
            jax.ShapeDtypeStruct(small.shape, F32),
        ),
        in_specs=[SMEM, SMEM] + [VMEM] * 3,
        out_specs=(VMEM,) * 4,
        scratch_shapes=[
            pltpu.VMEM((tile_size * tiles,) + back.shape[1:], BF16),
            pltpu.VMEM(acc.shape, F32),
            pltpu.VMEM(acc.shape, BF16),
            pltpu.VMEM((rows, 16, 128), BF16),
            pltpu.VMEM(acc.shape, BF16),
            pltpu.VMEM((slots,) + small.shape, F32),
            dma((tile_size - 1,)),
            dma((tile_size - 1,)),
            dma((sems,)),
            dma((sems,)),
            dma((sems,)),
            dma((sems,)),
            dma((slots,)),
            dma((slots,)),
        ],
        compiler_params=pltpu.CompilerParams(
            collective_id=1, has_side_effects=True, vmem_limit_bytes=60 * 2**20
        ),
        name="grad_sum",
    )(seam, corner, back, acc, small)


def rim_kernel(side, table_ref, xg_in, xg_ref):
    last = side - 1
    cells = side * side
    width = table_ref.shape[1]
    cell = iota((cells, 1), 0)
    i = cell // side
    j = cell % side
    r = iota((cells, width), 1)
    rim = None
    for s, (on, p) in enumerate(((i == 0, j), (j == last, i), (i == last, j), (j == 0, i))):
        hit = r == jnp.where(on, s * side + p, -1)
        rim = hit if rim is None else rim | hit
    for k, cell_k in enumerate((0, last, cells - 1, cells - side)):
        rim = rim | (r == jnp.where(cell == cell_k, SIDES * side + k, -1))
    rim = one_hot(rim)
    xg_ref[0] = xg_in[0] + dot(rim, table_ref[0])


def add_rims(xg, table):
    tiles, cells, channels = xg.shape
    block = pl.BlockSpec((1, cells, channels), lambda t: (t, 0, 0))
    return pl.pallas_call(
        functools.partial(rim_kernel, math.isqrt(cells)),
        grid=(tiles,),
        out_shape=jax.ShapeDtypeStruct(xg.shape, F32),
        in_specs=[pl.BlockSpec((1,) + table.shape[1:], lambda t: (t, 0, 0)), block],
        out_specs=block,
        compiler_params=pltpu.CompilerParams(vmem_limit_bytes=60 * 2**20),
        name="add_rims",
    )(table, xg)


def body(
    inputs,
    grad_out,
    seam_links,
    corner_links,
    dw_weight,
    norm_gain,
    w_in,
    bias_in,
    w_out,
    layer_scale,
):
    samples, local, side, _, channels = inputs.shape
    tiles = samples * local
    x = inputs.reshape(tiles, side * side, channels)
    g = grad_out.reshape(tiles, side * side, channels)
    cell_total = lax.axis_size("tile") * lax.axis_size("rep") * tiles * side * side
    factor = 1.0 / math.sqrt(cell_total)
    strips = gather_halos(x)
    out, xg, back, acc, small = compute(
        seam_links,
        corner_links,
        strips,
        x,
        g,
        dw_weight.T,
        norm_gain[None],
        w_in,
        bias_in[None],
        w_out,
        layer_scale[None],
    )
    table, gwi, gwo, total = finish(seam_links, corner_links, side, back, acc, small, factor)
    xg = add_rims(xg, table)
    return (
        out.reshape(inputs.shape),
        xg.reshape(inputs.shape),
        total[0:9].T,
        total[9],
        gwi,
        total[11 : 11 + w_in.shape[1] // channels].reshape(-1),
        gwo,
        total[10],
    )


def solution(mesh):
    placed = (
        P("rep", "tile", None, None, None),
        P("rep", "tile", None, None, None),
        P("tile", None, None),
        P("tile", None, None),
        P(),
        P(),
        P(),
        P(),
        P(),
        P(),
    )
    return jax.shard_map(
        body,
        mesh=mesh,
        in_specs=placed,
        out_specs=(
            P("rep", "tile", None, None, None),
            P("rep", "tile", None, None, None),
            P(),
            P(),
            P(),
            P(),
            P(),
            P(),
        ),
        check_vma=False,
    )
```
